32 devices in a mesh: section: 8 (over z, x), dp: 4 (over y, core).
Axes of the slice: x: 2, y: 2, z: 4, core: 2. Of those that a mesh axis runs over, the one named last changes fastest.
Arguments:
- acts: bfloat16 [8, 512, 2048], P('section', 'dp'), may hold values from -12 to 12
- weights: bfloat16 [8, 2048, 2048], P('section', 'dp'), may hold values from -6 to 6
- cotangent: bfloat16 [8, 512, 2048], P('section', 'dp'), may hold values from -20 to 20, as said below
Outputs:
- shadow: bfloat16 [8, 512, 2048], P('section', 'dp')
- back_grad: bfloat16 [8, 512, 2048], P('section', 'dp')
- successor_weights: bfloat16 [8, 2048, 2048], P('section', 'dp')
The draws below stay inside these ranges and needn't reach their ends.
Inputs may be any that keep to these rules, and one draw needn't show every extreme that they name: `cotangent`: entries of order one; the typical size differs from section to section.
All inputs are finite; a program needn't handle non-finite values.
Results may differ from the reference program's by a relative error of at most 0.0047.
Values may be sent and summed in bfloat16 or wider, within the bound.
A program may use at most 64 MiB of HBM per device.

```python
import jax
import jax.numpy as jnp
from jax import lax

D = 2048
SECTIONS = 8
TOKENS = 512


def draw_acts(key, part):
    key = jax.random.fold_in(key, 11)
    phase = jax.random.uniform(jax.random.fold_in(key, 1), (), jnp.float32, 0.0, 1.0)
    place = jnp.mod(jnp.arange(D, dtype=jnp.float32) / jnp.float32(D) + phase, 1.0)
    rough = jax.random.uniform(jax.random.fold_in(key, 2), (D,), jnp.float32, -0.35, 0.35)
    column = jnp.exp(jnp.log(jnp.float32(10.0)) * place + rough) / 4.83
    base = jnp.clip(jax.random.normal(jax.random.fold_in(key, 3), (SECTIONS, TOKENS, D), jnp.float32), -4.0, 4.0)
    return jnp.clip((base + 0.3) * column[None, None, :], -12.0, 12.0).astype(jnp.bfloat16)


def draw_cotangent(key, part):
    key = jax.random.fold_in(key, 7)
    base = jax.random.normal(key, (SECTIONS, TOKENS, D), jnp.float32)
    rise = 1.0 + 2.0 * jnp.arange(SECTIONS, dtype=jnp.float32) / jnp.float32(max(SECTIONS - 1, 1))
    values = base * rise[:, None, None]
    shared = jax.random.normal(jax.random.fold_in(key, 2), (SECTIONS, 1, D), jnp.float32)
    values = values + 0.35 * shared * rise[:, None, None]
    return jnp.clip(values, -20.0, 20.0).astype(jnp.bfloat16)


def steps_of(stream_key, extent, pieces, low, top_value):
    loudness, own = 1.0, jax.random.fold_in(stream_key, 6)
    for position, shards_of in pieces:
        heights = jnp.exp(jax.random.uniform(jax.random.fold_in(own, position), (shards_of,), jnp.float32, low / len(pieces), top_value / len(pieces)))
        loudness = loudness * jnp.repeat(heights, extent[position] // shards_of).reshape([-1 if axis == position else 1 for axis in range(len(extent))])
    return loudness


def noise(rng, extent, scale, limit, pieces=(), kind=jnp.bfloat16):
    gain = steps_of(rng, extent, pieces, -0.22, 0.18) if pieces else 1.0
    drawn = jax.random.normal(rng, extent, jnp.float32) * scale * gain
    return jnp.minimum(jnp.maximum(drawn, -limit), limit).astype(kind)


def setup_inputs(seed: int = 0) -> dict:
    seeds = jax.random.split(jax.random.key(seed), 4)
    acts = draw_acts(jax.random.fold_in(seeds[3], 71), 0)
    weights = noise(seeds[1], (SECTIONS, D, D), 1.0, 6.0, ((0, 8), (1, 4)))
    cotangent = draw_cotangent(jax.random.fold_in(seeds[3], 71), 0)
    return {"acts": acts, "weights": weights, "cotangent": cotangent}


step_rate = 0.5

def gelu_slope(pre):
    return jax.jvp(jax.nn.gelu, (pre,), (jnp.ones_like(pre),))[1]

def layer(inputs, matrix):
    pre = jnp.dot(inputs, matrix, preferred_element_type=jnp.float32) / jnp.sqrt(jnp.float32(D))
    return ((inputs.astype(jnp.float32) + jax.nn.gelu(pre)).astype(jnp.bfloat16), pre)

def one_section(packed):
    inputs, matrix, upstream = packed
    out_act, pre = layer(inputs, matrix)
    pregrad = (upstream.astype(jnp.float32) * gelu_slope(pre)).astype(jnp.bfloat16)
    spread = lax.dot_general(pregrad, matrix, (((1,), (1,)), ((), ())), preferred_element_type=jnp.float32)
    input_grad = (upstream.astype(jnp.float32) + spread / jnp.sqrt(jnp.float32(D))).astype(jnp.bfloat16)
    wgrad = lax.dot_general(inputs, pregrad, (((0,), (0,)), ((), ())), preferred_element_type=jnp.float32)
    return (out_act, input_grad, wgrad / jnp.sqrt(jnp.float32(D)))

def reference(acts, weights, cotangent):
    out_act, input_grad, wgrad = lax.map(one_section, (acts, weights, cotangent))
    energy = jnp.sum(wgrad * wgrad)
    scale = step_rate / jnp.sqrt(energy / jnp.float32(SECTIONS * D * D) + 1e-05)
    updated = (weights.astype(jnp.float32) - scale * wgrad).astype(jnp.bfloat16)
    front = lax.map(lambda pair: layer(pair[0], pair[1])[0], (out_act[:-1], weights[1:]))
    zero_rows = jnp.zeros((1, TOKENS, D), jnp.bfloat16)
    shadow = jnp.concatenate([front, zero_rows], axis=0)
    back_grad = jnp.concatenate([input_grad[1:], zero_rows], axis=0)
    successor_weights = jnp.concatenate([updated[1:], jnp.zeros((1, D, D), jnp.bfloat16)], axis=0)
    return (shadow, back_grad, successor_weights)
```

```python
import functools
import math

import jax
import jax.numpy as jnp
from jax import lax
from jax.experimental import pallas as pl
from jax.experimental.pallas import tpu as pltpu
from jax.sharding import PartitionSpec as P

MESH = pl.DeviceIdType.MESH
step_rate = 0.5
GELU_A = math.sqrt(2.0 / math.pi)
GELU_B = 0.044715
F32 = jnp.float32
BF16 = jnp.bfloat16


def kernel(
    cfg, acts, w, cot, shadow, back, succ,
    wp, wn, xg, xn, ah, ch, cn, p1s, p1r, p2s, p2r, acc, oh, og, pgo, pgn, xt, wg,
    sps, spr, shs, e1, e2, es, ssem, rsem, lsem,
):
    S, n, t, D = cfg
    r, pairs, h = D // n, n // 2, D // 2
    R, tt, T = 2 * r, 2 * t, n * t
    half_pairs = max(pairs // 2, 1)
    inv_root = F32(1.0 / math.sqrt(D))
    s = lax.axis_index("section")
    j = lax.axis_index("dp")
    q, c = j // 2, j % 2
    other = 1 - c
    partner = (s, 2 * q + other)
    has_next = s < S - 1
    has_prev = s > 0
    first = s == 0
    prev = (lax.max(s - 1, 0), j)

    def rows(start, size):
        return pl.ds(pl.multiple_of(start, math.gcd(size, 128)), size)

    def cols(start, size):
        return pl.ds(pl.multiple_of(start, 128), size)

    def mate(d):
        return lax.rem(q + d, pairs)

    def source(d):
        return lax.rem(q - d + pairs, pairs)

    counts = {"s": 0, "r": 0}
    pending = []

    def fresh(kind, many=1):
        first_index = counts[kind]
        counts[kind] += many
        return first_index

    def when(pred, f):
        if pred is None:
            f()
        else:
            pl.when(pred)(f)

    def send(src, dst, recv_index, device, pred=None):
        index = fresh("s")

        def make():
            return pltpu.make_async_remote_copy(
                src_ref=src(), dst_ref=dst(), send_sem=ssem.at[index],
                recv_sem=rsem.at[recv_index], device_id=device, device_id_type=MESH,
            )

        when(pred, lambda: make().start())
        pending.append((pred, lambda: make().wait_send()))

    def recv(dst, recv_index):
        pltpu.make_async_remote_copy(
            src_ref=dst, dst_ref=dst, send_sem=ssem.at[0],
            recv_sem=rsem.at[recv_index], device_id=partner, device_id_type=MESH,
        ).wait_recv()

    barrier = pltpu.get_barrier_semaphore()
    for d in range(1, n):
        pl.semaphore_signal(barrier, inc=1, device_id=(s, lax.rem(j + d, n)), device_id_type=MESH)
    for d in range(1, S):
        pl.semaphore_signal(barrier, inc=1, device_id=(lax.rem(s + d, S), j), device_id_type=MESH)
    pl.semaphore_wait(barrier, (n - 1) + (S - 1))

    xd, xf = fresh("r", pairs), fresh("r", pairs)
    for d in range(1, pairs):
        send(lambda d=d: acts.at[:, cols(mate(d) * R, R)], lambda: xg.at[rows(j * t, t), :],
             xd + d, (s, 2 * mate(d) + c))
    send(lambda: acts.at[:, cols(q * R, R)], lambda: xg.at[rows(j * t, t), :], xf, partner)
    wpr = fresh("r")
    send(lambda: w, lambda: wp.at[rows(c * r, r), :], wpr, partner)
    ahr, chr_ = fresh("r"), fresh("r")
    send(lambda: acts.at[:, cols(other * h, h)], lambda: ah.at[rows(c * t, t), :], ahr, partner)
    send(lambda: cot.at[:, cols(other * h, h)], lambda: ch.at[rows(c * t, t), :], chr_, partner)
    wnr, wnf, xnr, pgr, cnr = (fresh("r") for _ in range(5))
    send(lambda: w, lambda: wn.at[rows(c * r, r), :], wnr, prev, has_prev)

    local = [
        pltpu.make_async_copy(w, wp.at[rows(c * r, r), :], lsem.at[0]),
        pltpu.make_async_copy(acts.at[:, cols(q * R, R)], xg.at[rows(j * t, t), :], lsem.at[1]),
        pltpu.make_async_copy(acts.at[:, cols(c * h, h)], ah.at[rows(c * t, t), :], lsem.at[2]),
        pltpu.make_async_copy(cot.at[:, cols(c * h, h)], ch.at[rows(c * t, t), :], lsem.at[3]),
    ]
    for copy in local:
        copy.start()
    for copy in local:
        copy.wait()

    def xrows(d, core):
        return xg.at[rows((2 * source(d) + core) * t, t), :]

    for d in range(1, pairs):
        recv(xrows(d, c), xd + d)
        send(lambda d=d: xrows(d, c), lambda d=d: xrows(d, c), xf + d, partner)
    for d in range(pairs):
        recv(xrows(d, other), xf + d)
    recv(wp.at[rows(other * r, r), :], wpr)
    send(lambda: xg.at[:, cols(c * r, r)], lambda: xn, xnr, prev, has_prev)

    step = min(256, h)

    def partials(gathered, matrix, out, landing, base, pred):
        for d in list(range(1, pairs)) + [0]:
            def body(k, carry, d=d):
                value = jnp.dot(
                    gathered[rows(mate(d) * tt, tt), :], matrix[:, cols(c * h + k * step, step)],
                    preferred_element_type=F32,
                )
                if d:
                    out[d, :, cols(k * step, step)] = value.astype(BF16)
                else:
                    acc[:, cols(k * step, step)] = value
                return carry

            when(pred, lambda body=body: lax.fori_loop(0, h // step, body, None))
            if d:
                send(lambda d=d: out.at[d], lambda d=d: landing.at[d], base + d,
                     (s, 2 * mate(d) + c), pred)

    f1 = fresh("r", pairs)
    partials(xg, wp, p1s, p1r, f1, None)
    recv(ah.at[rows(other * t, t), :], ahr)
    recv(ch.at[rows(other * t, t), :], chr_)
    for d in range(1, pairs):
        recv(p1r.at[d], f1 + d)

    def total(landing, here):
        pre = acc[here, :]
        for d in range(1, pairs):
            pre += landing[d, here, :].astype(F32)
        return pre * inv_root

    def tanh_of(pre):
        return jnp.tanh(F32(GELU_A) * (pre + F32(GELU_B) * (pre * pre * pre)))

    def act_body(i, carry):
        here = rows(i * 16, 16)
        pre = total(p1r, here)
        th = tanh_of(pre)
        oh[here, :] = (ah[here, :].astype(F32) + 0.5 * pre * (1.0 + th)).astype(BF16)
        slope = 0.5 * (1.0 + th) + 0.5 * pre * (1.0 - th * th) * (
            F32(GELU_A) * (1.0 + F32(3.0 * GELU_B) * (pre * pre)))
        pgo[c, rows(q * tt + i * 16, 16), :] = (ch[here, :].astype(F32) * slope).astype(BF16)
        return carry

    lax.fori_loop(0, tt // 16, act_body, None)

    def block(buf, half, qq):
        return buf.at[half, rows(qq * tt, tt), :]

    send(lambda: block(pgo, c, q), lambda: block(pgn, c, q), pgr, prev, has_prev)
    od, of, nd, nf = (fresh("r", pairs) for _ in range(4))

    def gather_start(buf, direct, forward, pred):
        for d in range(1, pairs):
            send(lambda: block(buf, c, q), lambda: block(buf, c, q), direct + d,
                 (s, 2 * mate(d) + c), pred)
        send(lambda: block(buf, c, q), lambda: block(buf, c, q), forward, partner, pred)

    def gather_end(buf, direct, forward, pred):
        for d in range(1, pairs):
            when(pred, lambda d=d: recv(block(buf, c, source(d)), direct + d))
            send(lambda d=d: block(buf, c, source(d)), lambda d=d: block(buf, c, source(d)),
                 forward + d, partner, pred)
        for d in range(pairs):
            when(pred, lambda d=d: recv(block(buf, other, source(d)), forward + d))

    gather_start(pgo, od, of, first)

    ogd, ogf = fresh("r", pairs), fresh("r", pairs)
    ours = q // half_pairs == c
    leads = jnp.logical_and(has_next, ours)
    follows = jnp.logical_and(has_next, jnp.logical_not(ours))

    def orows(qq):
        return og.at[rows(qq * tt, tt), :]

    for m in range(half_pairs):
        qq = c * half_pairs + m
        send(lambda m=m: oh.at[:, cols(m * R, R)], lambda: orows(q), ogd + q, (s, 2 * qq + c),
             jnp.logical_and(has_next, qq != q))
    send(lambda: cot, lambda: cn, cnr, prev, has_prev)

    @pl.when(leads)
    def _():
        copy = pltpu.make_async_copy(
            oh.at[:, cols(lax.rem(q, half_pairs) * R, R)], orows(q), lsem.at[0])
        copy.start()
        copy.wait()

    send(lambda: orows(q), lambda: orows(q), ogf, partner, leads)
    for d in range(1, pairs):
        when(leads, lambda d=d: recv(orows(source(d)), ogd + source(d)))
        send(lambda d=d: orows(source(d)), lambda d=d: orows(source(d)), ogf + d, partner, leads)
    for d in range(pairs):
        when(follows, lambda d=d: recv(orows(source(d)), ogf + d))

    wstep = min(256, h)

    def wgrad(buf, store):
        def body(k, total_sq):
            total_sq = total_sq
            for half in range(2):
                value = jnp.dot(xt[...], buf[half, :, cols(k * wstep, wstep)],
                                preferred_element_type=F32) * inv_root
                if store:
                    wg[:, cols(half * h + k * wstep, wstep)] = value
                total_sq = total_sq + jnp.sum(
                    (value * value).reshape(r // 8, 8, wstep), axis=0)
            return total_sq

        total_sq = lax.fori_loop(0, h // wstep, body, jnp.zeros((8, wstep), F32))
        tile = total_sq[:, :128]
        for k in range(1, wstep // 128):
            tile = tile + total_sq[:, k * 128:(k + 1) * 128]
        es[0] = es[0] + tile

    es[0] = jnp.zeros((8, 128), F32)
    gather_end(pgo, od, of, first)

    @pl.when(first)
    def _():
        xt[...] = jnp.transpose(xg[:, cols(c * r, r)])
        wgrad(pgo, False)

    @pl.when(has_next)
    def _():
        recv(block(pgn, c, q), pgr)

    gather_start(pgn, nd, nf, has_next)

    @pl.when(has_next)
    def _():
        recv(xn, xnr)
        xt[...] = jnp.transpose(xn[...])

    gather_end(pgn, nd, nf, has_next)

    @pl.when(has_next)
    def _():
        wgrad(pgn, True)

    e1r = fresh("r", n)
    for d in range(1, n):
        send(lambda: es.at[0], lambda d=d: e1.at[d], e1r + d, (s, lax.rem(j + d, n)))
    sum1 = es[0]
    for d in range(1, n):
        recv(e1.at[d], e1r + d)
        sum1 = sum1 + e1[d]
    es[1] = sum1
    e2r = fresh("r", S)
    for d in range(1, S):
        send(lambda: es.at[1], lambda d=d: e2.at[d], e2r + d, (lax.rem(s + d, S), j))

    own_rows = rows(c * r, r)

    @pl.when(has_next)
    def _():
        recv(wn.at[own_rows, :], wnr)

    send(lambda: wn.at[own_rows, :], lambda: wn.at[own_rows, :], wnf, partner, has_next)
    spr_base = fresh("r", n)

    def tile_of(dd):
        return sps.at[dd]

    for d in list(range(1, pairs)) + [0]:
        def spread(d=d):
            value = jnp.zeros((tt, r), F32)
            for half in range(2):
                value = value + lax.dot_general(
                    pgn[half, rows(mate(d) * tt, tt), :], wn[own_rows, half * h:(half + 1) * h],
                    (((1,), (1,)), ((), ())), preferred_element_type=F32)
            sps[2 * d] = (value[:t] * inv_root).astype(BF16)
            sps[2 * d + 1] = (value[t:] * inv_root).astype(BF16)

        when(has_next, spread)
        for core in range(2):
            target = 2 * mate(d) + core
            mine = target == j
            send(lambda d=d, core=core: sps.at[2 * d + core], lambda: spr.at[:, cols(j * r, r)],
                 spr_base + j, (s, target),
                 has_next if d else jnp.logical_and(has_next, jnp.logical_not(mine)))

    @pl.when(has_next)
    def _():
        copy = pltpu.make_async_copy(sps.at[c], spr.at[:, cols(j * r, r)], lsem.at[0])
        copy.start()
        copy.wait()
        recv(wn.at[rows(other * r, r), :], wnf)

    f2 = fresh("r", pairs)
    partials(og, wn, p2s, p2r, f2, has_next)

    sum2 = es[1]
    for d in range(1, S):
        recv(e2.at[d], e2r + d)
        sum2 = sum2 + e2[d]
    energy = jnp.sum(jnp.sum(sum2, axis=0, keepdims=True), axis=1, keepdims=True)
    scale = step_rate / jnp.sqrt(energy / F32(S * D * D) + F32(1e-05))

    @pl.when(has_next)
    def _():
        def update(i, carry):
            here = rows(i * 16, 16)
            old = wn[rows(c * r + i * 16, 16), :].astype(F32)
            succ[here, :] = (old - scale * wg[here, :]).astype(BF16)
            return carry

        lax.fori_loop(0, r // 16, update, None)
        for d in range(1, n):
            owner = lax.rem(j + d, n)
            recv(spr.at[:, cols(owner * r, r)], spr_base + owner)
        recv(cn, cnr)

        def add(i, carry):
            here = rows(i * 16, 16)
            back[here, :] = (cn[here, :].astype(F32) + spr[here, :].astype(F32)).astype(BF16)
            return carry

        lax.fori_loop(0, t // 16, add, None)
        for d in range(1, pairs):
            recv(p2r.at[d], f2 + d)

        def shade(i, carry):
            here = rows(i * 16, 16)
            pre = total(p2r, here)
            shs[here, :] = (oh[here, :].astype(F32)
                            + 0.5 * pre * (1.0 + tanh_of(pre))).astype(BF16)
            return carry

        lax.fori_loop(0, tt // 16, shade, None)

    shr = fresh("r")
    send(lambda: shs.at[rows(other * t, t), :], lambda: shadow.at[:, cols(c * h, h)], shr,
         partner, has_next)

    @pl.when(has_next)
    def _():
        copy = pltpu.make_async_copy(
            shs.at[rows(c * t, t), :], shadow.at[:, cols(c * h, h)], lsem.at[0])
        copy.start()
        copy.wait()
        recv(shadow.at[:, cols(other * h, h)], shr)

    @pl.when(jnp.logical_not(has_next))
    def _():
        def clear(i, carry):
            succ[rows(i * 16, 16), :] = jnp.zeros((16, D), BF16)
            return carry

        def clear_tokens(i, carry):
            shadow[rows(i * 16, 16), :] = jnp.zeros((16, D), BF16)
            back[rows(i * 16, 16), :] = jnp.zeros((16, D), BF16)
            return carry

        lax.fori_loop(0, r // 16, clear, None)
        lax.fori_loop(0, t // 16, clear_tokens, None)

    for pred, wait in pending:
        when(pred, wait)


def per_device(S, n, acts, weights, cotangent):
    t, D = acts.shape[1:]
    r, pairs, h = D // n, n // 2, D // 2
    R, tt, T = 2 * r, 2 * t, n * t
    sems = 10 * pairs + 4 * n + 2 * S + 24
    vmem = pl.BlockSpec(memory_space=pltpu.VMEM)
    shadow, back, succ = pl.pallas_call(
        functools.partial(kernel, (S, n, t, D)),
        out_shape=(
            jax.ShapeDtypeStruct((t, D), BF16),
            jax.ShapeDtypeStruct((t, D), BF16),
            jax.ShapeDtypeStruct((r, D), BF16),
        ),
        in_specs=[vmem] * 3,
        out_specs=(vmem,) * 3,
        scratch_shapes=[
            pltpu.VMEM((R, D), BF16),
            pltpu.VMEM((R, D), BF16),
            pltpu.VMEM((T, R), BF16),
            pltpu.VMEM((T, r), BF16),
            pltpu.VMEM((tt, h), BF16),
            pltpu.VMEM((tt, h), BF16),
            pltpu.VMEM((t, D), BF16),
            pltpu.VMEM((pairs, tt, h), BF16),
            pltpu.VMEM((pairs, tt, h), BF16),
            pltpu.VMEM((pairs, tt, h), BF16),
            pltpu.VMEM((pairs, tt, h), BF16),
            pltpu.VMEM((tt, h), F32),
            pltpu.VMEM((tt, h), BF16),
            pltpu.VMEM((T, R), BF16),
            pltpu.VMEM((2, T, h), BF16),
            pltpu.VMEM((2, T, h), BF16),
            pltpu.VMEM((r, T), BF16),
            pltpu.VMEM((r, D), F32),
            pltpu.VMEM((n, t, r), BF16),
            pltpu.VMEM((t, D), BF16),
            pltpu.VMEM((tt, h), BF16),
            pltpu.VMEM((n, 8, 128), F32),
            pltpu.VMEM((S, 8, 128), F32),
            pltpu.VMEM((2, 8, 128), F32),
            pltpu.SemaphoreType.DMA((sems,)),
            pltpu.SemaphoreType.DMA((sems,)),
            pltpu.SemaphoreType.DMA((4,)),
        ],
        compiler_params=pltpu.CompilerParams(
            collective_id=0, has_side_effects=True, vmem_limit_bytes=60 * 1024 * 1024
        ),
        name="relay",
    )(acts[0], weights[0], cotangent[0])
    return shadow[None], back[None], succ[None]


def solution(mesh):
    spec = P("section", "dp", None)
    return jax.shard_map(
        functools.partial(per_device, mesh.shape["section"], mesh.shape["dp"]),
        mesh=mesh,
        in_specs=(spec, spec, spec),
        out_specs=(spec, spec, spec),
        check_vma=False,
    )
```

```python
import functools
import math

import jax
import jax.numpy as jnp
from jax import lax
from jax.experimental import pallas as pl
from jax.experimental.pallas import tpu as pltpu
from jax.sharding import PartitionSpec as P

MESH = pl.DeviceIdType.MESH
step_rate = 0.5
GELU_A = math.sqrt(2.0 / math.pi)
GELU_B = 0.044715
F32 = jnp.float32
BF16 = jnp.bfloat16


def kernel(
    cfg, acts, w, cot, shadow, back, succ,
    wp, wn, xg, xn, ah, ch, cn, p1s, p1r, p2s, p2r, acc, oh, og, pgo, pgn, xt, wg,
    sps, spr, shs, su, bk, e1, e2, es, ssem, rsem, lsem,
):
    S, n, t, D = cfg
    r, pairs, h = D // n, n // 2, D // 2
    R, tt, T = 2 * r, 2 * t, n * t
    half_pairs = max(pairs // 2, 1)
    pieces = 4
    piece = h // pieces
    inv_root = F32(1.0 / math.sqrt(D))
    s = lax.axis_index("section")
    j = lax.axis_index("dp")
    q, c = j // 2, j % 2
    other = 1 - c
    partner = (s, 2 * q + other)
    has_next = s < S - 1
    has_prev = s > 0
    first = s == 0
    prev = (lax.max(s - 1, 0), j)

    def rows(start, size):
        return pl.ds(pl.multiple_of(start, math.gcd(size, 128)), size)

    def cols(start, size):
        return pl.ds(pl.multiple_of(start, 128), size)

    def mate(d):
        return lax.rem(q + d, pairs)

    def source(d):
        return lax.rem(q - d + pairs, pairs)

    counts = {"s": 0, "r": 0}
    pending = []

    def fresh(kind, many=1):
        first_index = counts[kind]
        counts[kind] += many
        return first_index

    def when(pred, f):
        if pred is None:
            f()
        else:
            pl.when(pred)(f)

    def send(src, dst, recv_index, device, pred=None):
        index = fresh("s")

        def make():
            return pltpu.make_async_remote_copy(
                src_ref=src(), dst_ref=dst(), send_sem=ssem.at[index],
                recv_sem=rsem.at[recv_index], device_id=device, device_id_type=MESH,
            )

        when(pred, lambda: make().start())
        pending.append((pred, lambda: make().wait_send()))

    def recv(dst, recv_index):
        pltpu.make_async_remote_copy(
            src_ref=dst, dst_ref=dst, send_sem=ssem.at[0],
            recv_sem=rsem.at[recv_index], device_id=partner, device_id_type=MESH,
        ).wait_recv()

    local = [
        pltpu.make_async_copy(w.at[:, cols(c * h, h)], wp.at[rows(c * r, r), :], lsem.at[0]),
        pltpu.make_async_copy(acts.at[:, cols(q * R, R)], xg.at[rows(j * t, t), :], lsem.at[1]),
        pltpu.make_async_copy(acts.at[:, cols(c * h, h)], ah.at[rows(c * t, t), :], lsem.at[2]),
        pltpu.make_async_copy(cot.at[:, cols(c * h, h)], ch.at[rows(c * t, t), :], lsem.at[3]),
    ]
    for copy in local:
        copy.start()

    barrier = pltpu.get_barrier_semaphore()
    for d in range(1, n):
        pl.semaphore_signal(barrier, inc=1, device_id=(s, lax.rem(j + d, n)), device_id_type=MESH)
    for d in range(1, S):
        pl.semaphore_signal(barrier, inc=1, device_id=(lax.rem(s + d, S), j), device_id_type=MESH)
    pl.semaphore_wait(barrier, (n - 1) + (S - 1))

    xd, xf = fresh("r", pairs), fresh("r", pairs)
    for d in range(1, pairs):
        send(lambda d=d: acts.at[:, cols(mate(d) * R, R)], lambda: xg.at[rows(j * t, t), :],
             xd + d, (s, 2 * mate(d) + c))
    send(lambda: acts.at[:, cols(q * R, R)], lambda: xg.at[rows(j * t, t), :], xf, partner)
    wpr = fresh("r")
    send(lambda: w.at[:, cols(other * h, h)], lambda: wp.at[rows(c * r, r), :], wpr, partner)
    ahr, chr_ = fresh("r"), fresh("r")
    send(lambda: acts.at[:, cols(other * h, h)], lambda: ah.at[rows(c * t, t), :], ahr, partner)
    send(lambda: cot.at[:, cols(other * h, h)], lambda: ch.at[rows(c * t, t), :], chr_, partner)
    xnr, pgr, cnr = (fresh("r") for _ in range(3))
    wnr, wnf = fresh("r", 2 * pieces), fresh("r", pieces)
    own_rows = rows(c * r, r)

    def relay_weights(ks):
        for k in ks:
            for half in range(2):
                here = pl.ds(half * h + k * piece, piece)
                send(lambda here=here: w.at[:, here], lambda here=here: wn.at[own_rows, here],
                     wnr + 2 * k + half, prev, has_prev)

    early, late = range(pieces // 2), range(pieces // 2, pieces)
    relay_weights(early)

    def xrows(d, core):
        return xg.at[rows((2 * source(d) + core) * t, t), :]

    for d in range(1, pairs):
        recv(xrows(d, c), xd + d)
        send(lambda d=d: xrows(d, c), lambda d=d: xrows(d, c), xf + d, partner)
    for d in range(pairs):
        recv(xrows(d, other), xf + d)
    recv(wp.at[rows(other * r, r), :], wpr)

    for copy in local:
        copy.wait()
    send(lambda: xg.at[:, cols(c * r, r)], lambda: xn, xnr, prev, has_prev)

    step = min(256, h)

    def product(gathered, matrix, at, out, d, k, width):
        value = jnp.dot(
            gathered[rows(mate(d) * tt, tt), :], matrix[:, cols(at + k * width, width)],
            preferred_element_type=F32,
        )
        if d:
            out[d, :, cols(k * width, width)] = value.astype(BF16)
        else:
            acc[:, cols(k * width, width)] = value

    f1 = fresh("r", pairs)
    for d in list(range(1, pairs)) + [0]:
        def body(k, carry, d=d):
            product(xg, wp, 0, p1s, d, k, step)
            return carry

        lax.fori_loop(0, h // step, body, None)
        if d:
            send(lambda d=d: p1s.at[d], lambda d=d: p1r.at[d], f1 + d, (s, 2 * mate(d) + c))
    recv(ah.at[rows(other * t, t), :], ahr)
    recv(ch.at[rows(other * t, t), :], chr_)
    for d in range(1, pairs):
        recv(p1r.at[d], f1 + d)

    def total(landing, here):
        pre = acc[here, :]
        for d in range(1, pairs):
            pre += landing[d, here, :].astype(F32)
        return pre * inv_root

    def tanh_of(pre):
        return jnp.tanh(F32(GELU_A) * (pre + F32(GELU_B) * (pre * pre * pre)))

    def act_body(i, carry):
        here = rows(i * 16, 16)
        pre = total(p1r, here)
        th = tanh_of(pre)
        oh[here, :] = (ah[here, :].astype(F32) + 0.5 * pre * (1.0 + th)).astype(BF16)
        slope = 0.5 * (1.0 + th) + 0.5 * pre * (1.0 - th * th) * (
            F32(GELU_A) * (1.0 + F32(3.0 * GELU_B) * (pre * pre)))
        pgo[c, rows(q * tt + i * 16, 16), :] = (ch[here, :].astype(F32) * slope).astype(BF16)
        return carry

    lax.fori_loop(0, tt // 16, act_body, None)

    def block(buf, half, qq):
        return buf.at[half, rows(qq * tt, tt), :]

    send(lambda: block(pgo, c, q), lambda: block(pgn, c, q), pgr, prev, has_prev)
    relayed = pending.pop()
    od, of, nd, nf = (fresh("r", pairs) for _ in range(4))

    def gather_start(buf, direct, forward, pred):
        for d in range(1, pairs):
            send(lambda: block(buf, c, q), lambda: block(buf, c, q), direct + d,
                 (s, 2 * mate(d) + c), pred)
        send(lambda: block(buf, c, q), lambda: block(buf, c, q), forward, partner, pred)

    def gather_end(buf, direct, forward, pred):
        for d in range(1, pairs):
            when(pred, lambda d=d: recv(block(buf, c, source(d)), direct + d))
            send(lambda d=d: block(buf, c, source(d)), lambda d=d: block(buf, c, source(d)),
                 forward + d, partner, pred)
        for d in range(pairs):
            when(pred, lambda d=d: recv(block(buf, other, source(d)), forward + d))

    gather_start(pgo, od, of, first)

    ogd, ogf = fresh("r", pairs), fresh("r", pairs)
    ours = q // half_pairs == c
    leads = jnp.logical_and(has_next, ours)
    follows = jnp.logical_and(has_next, jnp.logical_not(ours))

    def orows(qq):
        return og.at[rows(qq * tt, tt), :]

    for m in range(half_pairs):
        qq = c * half_pairs + m
        send(lambda m=m: oh.at[:, cols(m * R, R)], lambda: orows(q), ogd + q, (s, 2 * qq + c),
             jnp.logical_and(has_next, qq != q))

    @pl.when(leads)
    def _():
        copy = pltpu.make_async_copy(
            oh.at[:, cols(lax.rem(q, half_pairs) * R, R)], orows(q), lsem.at[0])
        copy.start()
        copy.wait()

    send(lambda: orows(q), lambda: orows(q), ogf, partner, leads)
    for d in range(1, pairs):
        when(leads, lambda d=d: recv(orows(source(d)), ogd + source(d)))
        send(lambda d=d: orows(source(d)), lambda d=d: orows(source(d)), ogf + d, partner, leads)
    for d in range(pairs):
        when(follows, lambda d=d: recv(orows(source(d)), ogf + d))

    f2 = fresh("r", pairs * pieces)

    def shadow_pieces(ks):
        for k in ks:
            @pl.when(has_next)
            def _(k=k):
                for half in range(2):
                    recv(wn.at[own_rows, half * h + k * piece:half * h + (k + 1) * piece],
                         wnr + 2 * k + half)

            theirs = cols(other * h + k * piece, piece)
            send(lambda theirs=theirs: wn.at[own_rows, theirs],
                 lambda theirs=theirs: wn.at[own_rows, theirs], wnf + k, partner, has_next)
        for k in ks:
            here = pl.ds(k * piece, piece)
            when(has_next, lambda k=k: recv(
                wn.at[rows(other * r, r), cols(c * h + k * piece, piece)], wnf + k))
            for d in list(range(1, pairs)) + [0]:
                when(has_next, lambda k=k, d=d: product(og, wn, c * h, p2s, d, k, piece))
                if d:
                    send(lambda d=d, here=here: p2s.at[d, :, here],
                         lambda d=d, here=here: p2r.at[d, :, here],
                         f2 + d * pieces + k, (s, 2 * mate(d) + c), has_next)

    wstep = min(256, h)

    def wgrad(buf, store):
        def body(k, total_sq):
            total_sq = total_sq
            for half in range(2):
                value = jnp.dot(xt[...], buf[half, :, cols(k * wstep, wstep)],
                                preferred_element_type=F32) * inv_root
                if store:
                    wg[:, cols(half * h + k * wstep, wstep)] = value
                total_sq = total_sq + jnp.sum(
                    (value * value).reshape(r // 8, 8, wstep), axis=0)
            return total_sq

        total_sq = lax.fori_loop(0, h // wstep, body, jnp.zeros((8, wstep), F32))
        tile = total_sq[:, :128]
        for k in range(1, wstep // 128):
            tile = tile + total_sq[:, k * 128:(k + 1) * 128]
        es[0] = es[0] + tile

    es[0] = jnp.zeros((8, 128), F32)
    shadow_pieces(early)

    @pl.when(has_next)
    def _():
        recv(block(pgn, c, q), pgr)

    gather_start(pgn, nd, nf, has_next)
    when(*relayed)
    relay_weights(late)
    send(lambda: cot, lambda: cn, cnr, prev, has_prev)
    gather_end(pgo, od, of, first)

    @pl.when(first)
    def _():
        xt[...] = jnp.transpose(xg[:, cols(c * r, r)])
        wgrad(pgo, False)

    @pl.when(has_next)
    def _():
        recv(xn, xnr)
        xt[...] = jnp.transpose(xn[...])

    gather_end(pgn, nd, nf, has_next)

    @pl.when(has_next)
    def _():
        wgrad(pgn, True)

    e1r = fresh("r", n)
    for d in range(1, n):
        send(lambda: es.at[0], lambda d=d: e1.at[d], e1r + d, (s, lax.rem(j + d, n)))
    sum1 = es[0]
    for d in range(1, n):
        recv(e1.at[d], e1r + d)
        sum1 = sum1 + e1[d]
    es[1] = sum1
    e2r = fresh("r", S)
    for d in range(1, S):
        send(lambda: es.at[1], lambda d=d: e2.at[d], e2r + d, (lax.rem(s + d, S), j))

    shadow_pieces(late)
    spr_base = fresh("r", n)

    def tile_of(dd):
        return sps.at[dd]

    for d in list(range(1, pairs)) + [0]:
        def spread(d=d):
            value = jnp.zeros((tt, r), F32)
            for half in range(2):
                value = value + lax.dot_general(
                    pgn[half, rows(mate(d) * tt, tt), :], wn[own_rows, half * h:(half + 1) * h],
                    (((1,), (1,)), ((), ())), preferred_element_type=F32)
            sps[2 * d] = (value[:t] * inv_root).astype(BF16)
            sps[2 * d + 1] = (value[t:] * inv_root).astype(BF16)

        when(has_next, spread)
        for core in range(2):
            target = 2 * mate(d) + core
            mine = target == j
            send(lambda d=d, core=core: sps.at[2 * d + core], lambda: spr.at[:, cols(j * r, r)],
                 spr_base + j, (s, target),
                 has_next if d else jnp.logical_and(has_next, jnp.logical_not(mine)))

    @pl.when(has_next)
    def _():
        copy = pltpu.make_async_copy(sps.at[c], spr.at[:, cols(j * r, r)], lsem.at[0])
        copy.start()
        copy.wait()

    sum2 = es[1]
    for d in range(1, S):
        recv(e2.at[d], e2r + d)
        sum2 = sum2 + e2[d]
    energy = jnp.sum(jnp.sum(sum2, axis=0, keepdims=True), axis=1, keepdims=True)
    scale = step_rate / jnp.sqrt(energy / F32(S * D * D) + F32(1e-05))

    @pl.when(has_next)
    def _():
        def update(i, carry):
            here = rows(i * 16, 16)
            old = wn[rows(c * r + i * 16, 16), :].astype(F32)
            su[here, :] = (old - scale * wg[here, :]).astype(BF16)
            return carry

        lax.fori_loop(0, r // 16, update, None)
        pltpu.make_async_copy(su, succ, lsem.at[1]).start()
        for d in range(1, n):
            owner = lax.rem(j + d, n)
            recv(spr.at[:, cols(owner * r, r)], spr_base + owner)
        recv(cn, cnr)

        def add(i, carry):
            here = rows(i * 16, 16)
            bk[here, :] = (cn[here, :].astype(F32) + spr[here, :].astype(F32)).astype(BF16)
            return carry

        lax.fori_loop(0, t // 16, add, None)
        pltpu.make_async_copy(bk, back, lsem.at[2]).start()
        for d in range(1, pairs):
            for k in range(pieces):
                recv(p2r.at[d, :, k * piece:(k + 1) * piece], f2 + d * pieces + k)

        def shade(i, carry):
            here = rows(i * 16, 16)
            pre = total(p2r, here)
            shs[here, :] = (oh[here, :].astype(F32)
                            + 0.5 * pre * (1.0 + tanh_of(pre))).astype(BF16)
            return carry

        lax.fori_loop(0, tt // 16, shade, None)

    shr = fresh("r")
    send(lambda: shs.at[rows(other * t, t), :], lambda: shadow.at[:, cols(c * h, h)], shr,
         partner, has_next)

    @pl.when(has_next)
    def _():
        copy = pltpu.make_async_copy(
            shs.at[rows(c * t, t), :], shadow.at[:, cols(c * h, h)], lsem.at[0])
        copy.start()
        copy.wait()
        recv(shadow.at[:, cols(other * h, h)], shr)

    @pl.when(jnp.logical_not(has_next))
    def _():
        def clear(i, carry):
            su[rows(i * 16, 16), :] = jnp.zeros((16, D), BF16)
            return carry

        def clear_tokens(i, carry):
            bk[rows(i * 16, 16), :] = jnp.zeros((16, D), BF16)
            return carry

        lax.fori_loop(0, r // 16, clear, None)
        lax.fori_loop(0, t // 16, clear_tokens, None)
        pltpu.make_async_copy(su, succ, lsem.at[1]).start()
        pltpu.make_async_copy(bk, back, lsem.at[2]).start()
        copy = pltpu.make_async_copy(bk, shadow, lsem.at[0])
        copy.start()
        copy.wait()

    pltpu.make_async_copy(su, succ, lsem.at[1]).wait()
    pltpu.make_async_copy(bk, back, lsem.at[2]).wait()
    for pred, wait in pending:
        when(pred, wait)


def hand_over(a, b, d, a_out, b_out, d_out):
    a_out[...] = a[...]
    b_out[...] = b[...]
    d_out[...] = d[...]


def per_device(S, n, acts, weights, cotangent):
    t, D = acts.shape[1:]
    r, pairs, h = D // n, n // 2, D // 2
    R, tt, T = 2 * r, 2 * t, n * t
    sems = 15 * pairs + 4 * n + 2 * S + 40
    held = pl.BlockSpec(memory_space=pl.ANY)
    shadow, back, succ = pl.pallas_call(
        functools.partial(kernel, (S, n, t, D)),
        out_shape=(
            jax.ShapeDtypeStruct((t, D), BF16),
            jax.ShapeDtypeStruct((t, D), BF16),
            jax.ShapeDtypeStruct((r, D), BF16),
        ),
        in_specs=[held] * 3,
        out_specs=(held,) * 3,
        scratch_shapes=[
            pltpu.VMEM((R, h), BF16),
            pltpu.VMEM((R, D), BF16),
            pltpu.VMEM((T, R), BF16),
            pltpu.VMEM((T, r), BF16),
            pltpu.VMEM((tt, h), BF16),
            pltpu.VMEM((tt, h), BF16),
            pltpu.VMEM((t, D), BF16),
            pltpu.VMEM((pairs, tt, h), BF16),
            pltpu.VMEM((pairs, tt, h), BF16),
            pltpu.VMEM((pairs, tt, h), BF16),
            pltpu.VMEM((pairs, tt, h), BF16),
            pltpu.VMEM((tt, h), F32),
            pltpu.VMEM((tt, h), BF16),
            pltpu.VMEM((T, R), BF16),
            pltpu.VMEM((2, T, h), BF16),
            pltpu.VMEM((2, T, h), BF16),
            pltpu.VMEM((r, T), BF16),
            pltpu.VMEM((r, D), F32),
            pltpu.VMEM((n, t, r), BF16),
            pltpu.VMEM((t, D), BF16),
            pltpu.VMEM((tt, h), BF16),
            pltpu.VMEM((r, D), BF16),
            pltpu.VMEM((t, D), BF16),
            pltpu.VMEM((n, 8, 128), F32),
            pltpu.VMEM((S, 8, 128), F32),
            pltpu.VMEM((2, 8, 128), F32),
            pltpu.SemaphoreType.DMA((sems,)),
            pltpu.SemaphoreType.DMA((sems,)),
            pltpu.SemaphoreType.DMA((4,)),
        ],
        compiler_params=pltpu.CompilerParams(
            collective_id=0, has_side_effects=True, vmem_limit_bytes=60 * 1024 * 1024
        ),
        name="relay",
    )(acts[0], weights[0], cotangent[0])
    blocks = [pl.BlockSpec((rows // 4, D), lambda i: (i, 0)) for rows in (t, t, r)]
    shadow, back, succ = pl.pallas_call(
        hand_over,
        grid=(4,),
        out_shape=tuple(jax.ShapeDtypeStruct(x.shape, x.dtype) for x in (shadow, back, succ)),
        in_specs=blocks,
        out_specs=tuple(blocks),
        name="hand_over",
    )(shadow, back, succ)
    return shadow[None], back[None], succ[None]


def solution(mesh):
    spec = P("section", "dp", None)
    return jax.shard_map(
        functools.partial(per_device, mesh.shape["section"], mesh.shape["dp"]),
        mesh=mesh,
        in_specs=(spec, spec, spec),
        out_specs=(spec, spec, spec),
        check_vma=False,
    )
```

```python
import functools
import math

import jax
import jax.numpy as jnp
from jax import lax
from jax.experimental import pallas as pl
from jax.experimental.pallas import tpu as pltpu
from jax.sharding import PartitionSpec as P

MESH = pl.DeviceIdType.MESH
step_rate = 0.5
GELU_A = math.sqrt(2.0 / math.pi)
GELU_B = 0.044715
F32 = jnp.float32
BF16 = jnp.bfloat16


def kernel(
    cfg, acts, w, cot, shadow, back, succ,
    wp, wn, xg, xn, ah, ch, cn, p1s, p1r, p2s, p2r, acc, oh, og, pgo, pgn, xt, wg,
    sps, spr, shs, su, bk, e1, e2, es, ssem, rsem, lsem,
):
    S, n, t, D = cfg
    r, pairs, h = D // n, n // 2, D // 2
    R, tt, T = 2 * r, 2 * t, n * t
    half_pairs = max(pairs // 2, 1)
    pieces = 4
    piece = h // pieces
    inv_root = F32(1.0 / math.sqrt(D))
    s = lax.axis_index("section")
    j = lax.axis_index("dp")
    q, c = j // 2, j % 2
    other = 1 - c
    partner = (s, 2 * q + other)
    has_next = s < S - 1
    has_prev = s > 0
    first = s == 0
    prev = (lax.max(s - 1, 0), j)

    def rows(start, size):
        return pl.ds(pl.multiple_of(start, math.gcd(size, 128)), size)

    def cols(start, size):
        return pl.ds(pl.multiple_of(start, 128), size)

    def mate(d):
        return lax.rem(q + d, pairs)

    def source(d):
        return lax.rem(q - d + pairs, pairs)

    counts = {"s": 0, "r": 0}
    pending = []

    def fresh(kind, many=1):
        first_index = counts[kind]
        counts[kind] += many
        return first_index

    def when(pred, f):
        if pred is None:
            f()
        else:
            pl.when(pred)(f)

    def send(src, dst, recv_index, device, pred=None):
        index = fresh("s")

        def make():
            return pltpu.make_async_remote_copy(
                src_ref=src(), dst_ref=dst(), send_sem=ssem.at[index],
                recv_sem=rsem.at[recv_index], device_id=device, device_id_type=MESH,
            )

        when(pred, lambda: make().start())
        pending.append((pred, lambda: make().wait_send()))

    def recv(dst, recv_index):
        pltpu.make_async_remote_copy(
            src_ref=dst, dst_ref=dst, send_sem=ssem.at[0],
            recv_sem=rsem.at[recv_index], device_id=partner, device_id_type=MESH,
        ).wait_recv()

    local = [
        pltpu.make_async_copy(w.at[:, cols(c * h, h)], wp.at[rows(c * r, r), :], lsem.at[0]),
        pltpu.make_async_copy(acts.at[:, cols(q * R, R)], xg.at[rows(j * t, t), :], lsem.at[1]),
        pltpu.make_async_copy(acts.at[:, cols(c * h, h)], ah.at[rows(c * t, t), :], lsem.at[2]),
        pltpu.make_async_copy(cot.at[:, cols(c * h, h)], ch.at[rows(c * t, t), :], lsem.at[3]),
    ]
    for copy in local:
        copy.start()

    barrier = pltpu.get_barrier_semaphore()
    for d in range(1, n):
        pl.semaphore_signal(barrier, inc=1, device_id=(s, lax.rem(j + d, n)), device_id_type=MESH)
    for d in range(1, S):
        pl.semaphore_signal(barrier, inc=1, device_id=(lax.rem(s + d, S), j), device_id_type=MESH)
    pl.semaphore_wait(barrier, (n - 1) + (S - 1))

    xd, xf = fresh("r", pairs), fresh("r", pairs)
    for d in range(1, pairs):
        send(lambda d=d: acts.at[:, cols(mate(d) * R, R)], lambda: xg.at[rows(j * t, t), :],
             xd + d, (s, 2 * mate(d) + c))
    send(lambda: acts.at[:, cols(q * R, R)], lambda: xg.at[rows(j * t, t), :], xf, partner)
    wpr = fresh("r")
    send(lambda: w.at[:, cols(other * h, h)], lambda: wp.at[rows(c * r, r), :], wpr, partner)
    ahr, chr_ = fresh("r"), fresh("r")
    send(lambda: acts.at[:, cols(other * h, h)], lambda: ah.at[rows(c * t, t), :], ahr, partner)
    send(lambda: cot.at[:, cols(other * h, h)], lambda: ch.at[rows(c * t, t), :], chr_, partner)
    xnr, cnr = fresh("r"), fresh("r")
    wnr, wnf = fresh("r", 2 * pieces), fresh("r", pieces)
    own_rows = rows(c * r, r)

    def relay_weights(ks):
        for k in ks:
            for half in range(2):
                here = pl.ds(half * h + k * piece, piece)
                send(lambda here=here: w.at[:, here], lambda here=here: wn.at[own_rows, here],
                     wnr + 2 * k + half, prev, has_prev)

    early, late = range(pieces // 2), range(pieces // 2, pieces)
    relay_weights(early)

    def xrows(d, core):
        return xg.at[rows((2 * source(d) + core) * t, t), :]

    for d in range(1, pairs):
        recv(xrows(d, c), xd + d)
        send(lambda d=d: xrows(d, c), lambda d=d: xrows(d, c), xf + d, partner)
    for d in range(pairs):
        recv(xrows(d, other), xf + d)
    recv(wp.at[rows(other * r, r), :], wpr)

    for copy in local:
        copy.wait()
    send(lambda: xg.at[:, cols(c * r, r)], lambda: xn, xnr, prev, has_prev)

    step = min(256, h)

    def product(gathered, matrix, at, out, d, k, width, lo=0, size=tt):
        value = jnp.dot(
            gathered[rows(mate(d) * tt + lo, size), :], matrix[:, cols(at + k * width, width)],
            preferred_element_type=F32,
        )
        if d:
            out[d, lo:lo + size, cols(k * width, width)] = value.astype(BF16)
        else:
            acc[lo:lo + size, cols(k * width, width)] = value

    f1 = fresh("r", 2 * pairs)
    for d in list(range(1, pairs)) + [0]:
        for u in range(2):
            def body(k, carry, d=d, u=u):
                product(xg, wp, 0, p1s, d, k, step, u * t, t)
                return carry

            lax.fori_loop(0, h // step, body, None)
            if d:
                part = slice(u * t, (u + 1) * t)
                send(lambda d=d, part=part: p1s.at[d, part], lambda d=d, part=part: p1r.at[d, part],
                     f1 + 2 * d + u, (s, 2 * mate(d) + c))
    recv(ah.at[rows(other * t, t), :], ahr)
    recv(ch.at[rows(other * t, t), :], chr_)

    def total(landing, here):
        pre = acc[here, :]
        for d in range(1, pairs):
            pre += landing[d, here, :].astype(F32)
        return pre * inv_root

    def tanh_of(pre):
        return jnp.tanh(F32(GELU_A) * (pre + F32(GELU_B) * (pre * pre * pre)))

    def act_body(i, carry):
        here = rows(i * 16, 16)
        pre = total(p1r, here)
        th = tanh_of(pre)
        oh[here, :] = (ah[here, :].astype(F32) + 0.5 * pre * (1.0 + th)).astype(BF16)
        slope = 0.5 * (1.0 + th) + 0.5 * pre * (1.0 - th * th) * (
            F32(GELU_A) * (1.0 + F32(3.0 * GELU_B) * (pre * pre)))
        pgo[c, rows(q * tt + i * 16, 16), :] = (ch[here, :].astype(F32) * slope).astype(BF16)
        return carry

    def block(buf, half, qq, u):
        return buf.at[half, rows(qq * tt + u * t, t), :]

    relayed = []
    pgr = fresh("r", 2)
    for u in range(2):
        for d in range(1, pairs):
            recv(p1r.at[d, u * t:(u + 1) * t], f1 + 2 * d + u)
        lax.fori_loop(u * (t // 16), (u + 1) * (t // 16), act_body, None)
        send(lambda u=u: block(pgo, c, q, u), lambda u=u: block(pgn, c, q, u), pgr + u, prev,
             has_prev)
        relayed.append(pending.pop())

    relay_weights(late)

    od, of, nd, nf = (fresh("r", 2 * pairs) for _ in range(4))

    def gather_start(buf, direct, forward, pred, u):
        here = lambda: block(buf, c, q, u)
        for d in range(1, pairs):
            send(here, here, direct + 2 * d + u, (s, 2 * mate(d) + c), pred)
        send(here, here, forward + u, partner, pred)

    def gather_end(buf, direct, forward, pred):
        for u in range(2):
            for d in range(1, pairs):
                here = lambda d=d, u=u: block(buf, c, source(d), u)
                when(pred, lambda d=d, u=u, here=here: recv(here(), direct + 2 * d + u))
                send(here, here, forward + 2 * d + u, partner, pred)
        for u in range(2):
            for d in range(pairs):
                when(pred, lambda d=d, u=u: recv(
                    block(buf, other, source(d), u), forward + 2 * d + u))

    gather_start(pgo, od, of, first, 0)
    gather_start(pgo, od, of, first, 1)

    ogd, ogf = fresh("r", pairs), fresh("r", pairs)
    ours = q // half_pairs == c
    leads = jnp.logical_and(has_next, ours)
    follows = jnp.logical_and(has_next, jnp.logical_not(ours))

    def orows(qq):
        return og.at[rows(qq * tt, tt), :]

    for m in range(half_pairs):
        qq = c * half_pairs + m
        send(lambda m=m: oh.at[:, cols(m * R, R)], lambda: orows(q), ogd + q, (s, 2 * qq + c),
             jnp.logical_and(has_next, qq != q))

    @pl.when(leads)
    def _():
        copy = pltpu.make_async_copy(
            oh.at[:, cols(lax.rem(q, half_pairs) * R, R)], orows(q), lsem.at[0])
        copy.start()
        copy.wait()

    send(lambda: orows(q), lambda: orows(q), ogf, partner, leads)
    for d in range(1, pairs):
        when(leads, lambda d=d: recv(orows(source(d)), ogd + source(d)))
        send(lambda d=d: orows(source(d)), lambda d=d: orows(source(d)), ogf + d, partner, leads)
    for d in range(pairs):
        when(follows, lambda d=d: recv(orows(source(d)), ogf + d))

    f2 = fresh("r", pairs * pieces)

    def shadow_pieces(ks):
        for k in ks:
            @pl.when(has_next)
            def _(k=k):
                for half in range(2):
                    recv(wn.at[own_rows, half * h + k * piece:half * h + (k + 1) * piece],
                         wnr + 2 * k + half)

            theirs = cols(other * h + k * piece, piece)
            send(lambda theirs=theirs: wn.at[own_rows, theirs],
                 lambda theirs=theirs: wn.at[own_rows, theirs], wnf + k, partner, has_next)
        for k in ks:
            here = pl.ds(k * piece, piece)
            when(has_next, lambda k=k: recv(
                wn.at[rows(other * r, r), cols(c * h + k * piece, piece)], wnf + k))
            for d in list(range(1, pairs)) + [0]:
                when(has_next, lambda k=k, d=d: product(og, wn, c * h, p2s, d, k, piece))
                if d:
                    send(lambda d=d, here=here: p2s.at[d, :, here],
                         lambda d=d, here=here: p2r.at[d, :, here],
                         f2 + d * pieces + k, (s, 2 * mate(d) + c), has_next)

    wstep = min(256, h)

    def wgrad(buf, store):
        def body(k, total_sq):
            total_sq = total_sq
            for half in range(2):
                value = jnp.dot(xt[...], buf[half, :, cols(k * wstep, wstep)],
                                preferred_element_type=F32) * inv_root
                if store:
                    wg[:, cols(half * h + k * wstep, wstep)] = value
                total_sq = total_sq + jnp.sum(
                    (value * value).reshape(r // 8, 8, wstep), axis=0)
            return total_sq

        total_sq = lax.fori_loop(0, h // wstep, body, jnp.zeros((8, wstep), F32))
        tile = total_sq[:, :128]
        for k in range(1, wstep // 128):
            tile = tile + total_sq[:, k * 128:(k + 1) * 128]
        es[0] = es[0] + tile

    es[0] = jnp.zeros((8, 128), F32)
    for u in range(2):
        when(has_next, lambda u=u: recv(block(pgn, c, q, u), pgr + u))
        gather_start(pgn, nd, nf, has_next, u)
        when(*relayed[u])
    send(lambda: cot, lambda: cn, cnr, prev, has_prev)

    gather_end(pgo, od, of, first)

    @pl.when(first)
    def _():
        xt[...] = jnp.transpose(xg[:, cols(c * r, r)])
        wgrad(pgo, False)

    @pl.when(has_next)
    def _():
        recv(xn, xnr)
        xt[...] = jnp.transpose(xn[...])

    gather_end(pgn, nd, nf, has_next)

    @pl.when(has_next)
    def _():
        wgrad(pgn, True)

    e1r = fresh("r", n)
    for d in range(1, n):
        send(lambda: es.at[0], lambda d=d: e1.at[d], e1r + d, (s, lax.rem(j + d, n)))
    sum1 = es[0]
    for d in range(1, n):
        recv(e1.at[d], e1r + d)
        sum1 = sum1 + e1[d]
    es[1] = sum1
    e2r = fresh("r", S)
    for d in range(1, S):
        send(lambda: es.at[1], lambda d=d: e2.at[d], e2r + d, (lax.rem(s + d, S), j))

    shadow_pieces(early)
    shadow_pieces(late)
    spr_base = fresh("r", n)

    def tile_of(dd):
        return sps.at[dd]

    for d in list(range(1, pairs)) + [0]:
        def spread(d=d):
            value = jnp.zeros((tt, r), F32)
            for half in range(2):
                value = value + lax.dot_general(
                    pgn[half, rows(mate(d) * tt, tt), :], wn[own_rows, half * h:(half + 1) * h],
                    (((1,), (1,)), ((), ())), preferred_element_type=F32)
            sps[2 * d] = (value[:t] * inv_root).astype(BF16)
            sps[2 * d + 1] = (value[t:] * inv_root).astype(BF16)

        when(has_next, spread)
        for core in range(2):
            target = 2 * mate(d) + core
            mine = target == j
            send(lambda d=d, core=core: sps.at[2 * d + core], lambda: spr.at[:, cols(j * r, r)],
                 spr_base + j, (s, target),
                 has_next if d else jnp.logical_and(has_next, jnp.logical_not(mine)))

    @pl.when(has_next)
    def _():
        copy = pltpu.make_async_copy(sps.at[c], spr.at[:, cols(j * r, r)], lsem.at[0])
        copy.start()
        copy.wait()

    sum2 = es[1]
    for d in range(1, S):
        recv(e2.at[d], e2r + d)
        sum2 = sum2 + e2[d]
    energy = jnp.sum(jnp.sum(sum2, axis=0, keepdims=True), axis=1, keepdims=True)
    scale = step_rate / jnp.sqrt(energy / F32(S * D * D) + F32(1e-05))

    @pl.when(has_next)
    def _():
        def update(i, carry):
            here = rows(i * 16, 16)
            old = wn[rows(c * r + i * 16, 16), :].astype(F32)
            su[here, :] = (old - scale * wg[here, :]).astype(BF16)
            return carry

        lax.fori_loop(0, r // 16, update, None)
        pltpu.make_async_copy(su, succ, lsem.at[1]).start()
        for d in range(1, n):
            owner = lax.rem(j + d, n)
            recv(spr.at[:, cols(owner * r, r)], spr_base + owner)
        recv(cn, cnr)

        def add(i, carry):
            here = rows(i * 16, 16)
            bk[here, :] = (cn[here, :].astype(F32) + spr[here, :].astype(F32)).astype(BF16)
            return carry

        lax.fori_loop(0, t // 16, add, None)
        pltpu.make_async_copy(bk, back, lsem.at[2]).start()
        for d in range(1, pairs):
            for k in range(pieces):
                recv(p2r.at[d, :, k * piece:(k + 1) * piece], f2 + d * pieces + k)

        def shade(i, carry):
            here = rows(i * 16, 16)
            pre = total(p2r, here)
            shs[here, :] = (oh[here, :].astype(F32)
                            + 0.5 * pre * (1.0 + tanh_of(pre))).astype(BF16)
            return carry

        lax.fori_loop(0, tt // 16, shade, None)

    shr = fresh("r")
    send(lambda: shs.at[rows(other * t, t), :], lambda: shadow.at[:, cols(c * h, h)], shr,
         partner, has_next)

    @pl.when(has_next)
    def _():
        copy = pltpu.make_async_copy(
            shs.at[rows(c * t, t), :], shadow.at[:, cols(c * h, h)], lsem.at[0])
        copy.start()
        copy.wait()
        recv(shadow.at[:, cols(other * h, h)], shr)

    @pl.when(jnp.logical_not(has_next))
    def _():
        def clear(i, carry):
            su[rows(i * 16, 16), :] = jnp.zeros((16, D), BF16)
            return carry

        def clear_tokens(i, carry):
            bk[rows(i * 16, 16), :] = jnp.zeros((16, D), BF16)
            return carry

        lax.fori_loop(0, r // 16, clear, None)
        lax.fori_loop(0, t // 16, clear_tokens, None)
        pltpu.make_async_copy(su, succ, lsem.at[1]).start()
        pltpu.make_async_copy(bk, back, lsem.at[2]).start()
        copy = pltpu.make_async_copy(bk, shadow, lsem.at[0])
        copy.start()
        copy.wait()

    pltpu.make_async_copy(su, succ, lsem.at[1]).wait()
    pltpu.make_async_copy(bk, back, lsem.at[2]).wait()
    for pred, wait in pending:
        when(pred, wait)


def hand_over(a, b, d, a_out, b_out, d_out):
    a_out[...] = a[...]
    b_out[...] = b[...]
    d_out[...] = d[...]


def per_device(S, n, acts, weights, cotangent):
    t, D = acts.shape[1:]
    r, pairs, h = D // n, n // 2, D // 2
    R, tt, T = 2 * r, 2 * t, n * t
    sems = 26 * pairs + 4 * n + 2 * S + 40
    held = pl.BlockSpec(memory_space=pl.ANY)
    shadow, back, succ = pl.pallas_call(
        functools.partial(kernel, (S, n, t, D)),
        out_shape=(
            jax.ShapeDtypeStruct((t, D), BF16),
            jax.ShapeDtypeStruct((t, D), BF16),
            jax.ShapeDtypeStruct((r, D), BF16),
        ),
        in_specs=[held] * 3,
        out_specs=(held,) * 3,
        scratch_shapes=[
            pltpu.VMEM((R, h), BF16),
            pltpu.VMEM((R, D), BF16),
            pltpu.VMEM((T, R), BF16),
            pltpu.VMEM((T, r), BF16),
            pltpu.VMEM((tt, h), BF16),
            pltpu.VMEM((tt, h), BF16),
            pltpu.VMEM((t, D), BF16),
            pltpu.VMEM((pairs, tt, h), BF16),
            pltpu.VMEM((pairs, tt, h), BF16),
            pltpu.VMEM((pairs, tt, h), BF16),
            pltpu.VMEM((pairs, tt, h), BF16),
            pltpu.VMEM((tt, h), F32),
            pltpu.VMEM((tt, h), BF16),
            pltpu.VMEM((T, R), BF16),
            pltpu.VMEM((2, T, h), BF16),
            pltpu.VMEM((2, T, h), BF16),
            pltpu.VMEM((r, T), BF16),
            pltpu.VMEM((r, D), F32),
            pltpu.VMEM((n, t, r), BF16),
            pltpu.VMEM((t, D), BF16),
            pltpu.VMEM((tt, h), BF16),
            pltpu.VMEM((r, D), BF16),
            pltpu.VMEM((t, D), BF16),
            pltpu.VMEM((n, 8, 128), F32),
            pltpu.VMEM((S, 8, 128), F32),
            pltpu.VMEM((2, 8, 128), F32),
            pltpu.SemaphoreType.DMA((sems,)),
            pltpu.SemaphoreType.DMA((sems,)),
            pltpu.SemaphoreType.DMA((4,)),
        ],
        compiler_params=pltpu.CompilerParams(
            collective_id=0, has_side_effects=True, vmem_limit_bytes=60 * 1024 * 1024
        ),
        name="relay",
    )(acts[0], weights[0], cotangent[0])
    blocks = [pl.BlockSpec((rows // 4, D), lambda i: (i, 0)) for rows in (t, t, r)]
    shadow, back, succ = pl.pallas_call(
        hand_over,
        grid=(4,),
        out_shape=tuple(jax.ShapeDtypeStruct(x.shape, x.dtype) for x in (shadow, back, succ)),
        in_specs=blocks,
        out_specs=tuple(blocks),
        name="hand_over",
    )(shadow, back, succ)
    return shadow[None], back[None], succ[None]


def solution(mesh):
    spec = P("section", "dp", None)
    return jax.shard_map(
        functools.partial(per_device, mesh.shape["section"], mesh.shape["dp"]),
        mesh=mesh,
        in_specs=(spec, spec, spec),
        out_specs=(spec, spec, spec),
        check_vma=False,
    )
```
